32 devices in a mesh: parts: 2 (over y), dp: 4 (over z), tensor: 4 (over x, core).
Axes of the slice: x: 2, y: 2, z: 4, core: 2. Of those that a mesh axis runs over, the one named last changes fastest.
Arguments:
- tokens: bfloat16 [2048, 8192], P(('parts', 'dp'), 'tensor'), parts along dimension 0, may hold values from -6 to 6
- query_weight: bfloat16 [8192, 8192], P('dp', 'tensor'), may hold values from -0.0625 to 0.0625
- down_weights: bfloat16 [64, 16, 8192], P('parts', None, 'tensor'), parts along dimension 0, may hold values from -0.0625 to 0.0625
- up_weights: bfloat16 [64, 16, 8192], P('parts', None, 'tensor'), parts along dimension 0, may hold values from -0.0625 to 0.0625
- cotangent: bfloat16 [2048, 8192], P(('parts', 'dp'), 'tensor'), parts along dimension 0, may hold values from -1.1953125 to 1.1953125
- adapter_of_block: int32 [16], P(('parts', 'dp')), parts along dimension 0, may hold values from 0 to 31
- block_live_count: int32 [16], P(('parts', 'dp')), parts along dimension 0, may hold values from 1 to 128, 768 in all
Outputs:
- query: bfloat16 [2048, 8192], P(('parts', 'dp'), 'tensor'), parts along dimension 0
- token_gradient: bfloat16 [2048, 8192], P(('parts', 'dp'), 'tensor'), parts along dimension 0
- grad_down: float32 [64, 16, 8192], P('parts', None, 'tensor'), parts along dimension 0
- grad_up: float32 [64, 16, 8192], P('parts', None, 'tensor'), parts along dimension 0
The draws below stay inside these ranges and needn't reach their ends.
There are 2 independent parts, one for each index of `parts`. The reference program is written for one: setup_inputs(seed, part) draws one part's arguments, and reference() takes and returns one part's arrays. A program takes and returns all parts, laid end to end along the dimension named above; an argument that names none is the same for every part. Nothing has to cross between parts.
Inputs may be any that keep to these rules, and one draw needn't show every extreme that they name: `block_live_count`: the counts of one part sum to three quarters of 1024, and some block is full.
All inputs are finite; a program needn't handle non-finite values.
Results may differ from the reference program's by a relative error of at most 0.012.
Values may be sent and summed in bfloat16 or wider, within the bound.
No kernel may reach another device: no remote copies, remote signals or barrier semaphores. Data moves between devices by JAX's collectives and lax.ppermute only.
A program may use at most 192 MiB of HBM per device.

```python
import math
import jax
import jax.numpy as jnp
import numpy as np
from jax import lax

MODEL_WIDTH = 8192
ADAPTER_RANK = 16
ADAPTER_COUNT = 32
BLOCK = 128
QUERY_WIDTH = 8192
BLOCKS = 8
TOKEN_SLOTS = 1024
N_TENSOR = 4


def with_ends(drawn, rng, least, high):
    dims = drawn.shape
    index_at = [jax.random.randint(jax.random.fold_in(rng, axis), (), 0, dims[axis]) for axis in range(len(dims))]
    drawn = drawn.at[tuple(index_at)].set(least)
    longest = dims.index(max(dims))
    index_at[longest] = (index_at[longest] + 1) % dims[longest]
    return drawn.at[tuple(index_at)].set(high)


def shard_levels(own_key, dims, split, smallest, high):
    gain, own = 1.0, jax.random.fold_in(own_key, 6)
    for dim, blocks in split:
        heights = jnp.exp(jax.random.uniform(jax.random.fold_in(own, dim), (blocks,), jnp.float32, smallest / len(split), high / len(split)))
        gain = gain * jnp.repeat(heights, dims[dim] // blocks).reshape([-1 if axis == dim else 1 for axis in range(len(dims))])
    return gain


def rank_bounds(count, skew):
    weights = [(1 << 20) // math.isqrt(grade ** skew) + 1 for grade in range(1, count + 1)]
    width = 1 + sum(weights) // (1 << 30)
    return np.cumsum(np.array([max(1, weight // width) for weight in weights]))


def skewed_ids(rng, extent, amount, lean):
    grid = rank_bounds(amount, lean)
    pick = jax.random.randint(jax.random.fold_in(rng, 1), extent, 0, int(grid[amount - 1]))
    rank = jnp.searchsorted(jnp.asarray(grid, jnp.int32), pick, side="right")
    return jax.random.permutation(jax.random.fold_in(rng, 2), amount)[rank].astype(jnp.int32)


def split_up(count, total, limit, slope):
    loads = [(1 << 20) // math.isqrt(rank ** slope) + 1 for rank in range(2, count + 1)]
    surplus, counts = total - limit - (count - 1), [1] * (count - 1)
    while surplus > 0:
        candidates = [i for i in range(count - 1) if counts[i] < limit]
        pool, remaining = sum([loads[i] for i in candidates]), surplus
        for i in candidates:
            extra = min(limit - counts[i], max(1, remaining * loads[i] // pool), surplus)
            counts[i] = counts[i] + extra
            surplus = surplus - extra
    return np.array([limit] + counts)


def uneven(rng, amount, total, most, skew):
    if amount == 2:
        one = jax.random.randint(rng, (), max(1, total - most), min(most, total - 1) + 1)
        return jnp.stack([one, total - one])
    tallies = jnp.asarray(split_up(amount, total, most, skew), jnp.int32)
    couples = (amount - 1) // 2
    donor, taker = tallies[1:1 + 2 * couples:2], tallies[2:2 + 2 * couples:2]
    slack = jnp.minimum(donor - 1, most - taker)
    moved = jax.random.randint(jax.random.fold_in(rng, 1), (couples,), 0, 1 << 20) % (slack + 1)
    tallies = tallies.at[1:1 + 2 * couples:2].set(donor - moved).at[2:2 + 2 * couples:2].set(taker + moved)
    return tallies[jax.random.permutation(jax.random.fold_in(rng, 2), amount)]


def normal_values(stream_key, extent, width, limit, cuts=(), kind=jnp.bfloat16):
    result = jax.random.normal(stream_key, extent, jnp.float32) * width
    if len(cuts) > 0:
        result = shard_levels(stream_key, extent, cuts, -0.22, 0.18) * result
    return jnp.clip(result, min=-limit, max=limit).astype(kind)


def setup_inputs(seed: int = 0, part: int = 0) -> dict:
    arg_keys = jax.random.split(jax.random.key(seed), 8)
    own_keys = jax.random.split(jax.random.fold_in(arg_keys[7], part), 8)
    tokens = normal_values(own_keys[0], (TOKEN_SLOTS, MODEL_WIDTH), 1.0, 6.0, ((0, 4), (1, 4)))
    query_weight = normal_values(arg_keys[1], (MODEL_WIDTH, QUERY_WIDTH), MODEL_WIDTH ** -0.5, 0.0625, ((0, 4), (1, 4)))
    down_weights = normal_values(own_keys[2], (ADAPTER_COUNT, ADAPTER_RANK, MODEL_WIDTH), MODEL_WIDTH ** -0.5, 0.0625, ((2, 4),))
    up_weights = normal_values(own_keys[3], (ADAPTER_COUNT, ADAPTER_RANK, QUERY_WIDTH), QUERY_WIDTH ** -0.5, 0.0625, ((2, 4),))
    cotangent = normal_values(own_keys[4], (TOKEN_SLOTS, QUERY_WIDTH), 0.2, 1.1953125, ((0, 4), (1, 4)))
    adapter_of_block = with_ends(skewed_ids(own_keys[5], (BLOCKS,), ADAPTER_COUNT, 2), jax.random.fold_in(own_keys[5], 3), 0, ADAPTER_COUNT - 1).astype(jnp.int32)
    block_live_count = uneven(own_keys[6], BLOCKS, 3 * BLOCKS * BLOCK // 4, BLOCK, 1).astype(jnp.int32)
    return {"tokens": tokens, "query_weight": query_weight, "down_weights": down_weights, "up_weights": up_weights, "cotangent": cotangent, "adapter_of_block": adapter_of_block, "block_live_count": block_live_count}


def reference(tokens, query_weight, down_weights, up_weights, cotangent, adapter_of_block, block_live_count):
    blocks_total = adapter_of_block.shape[0]
    input_blocks = tokens.reshape(blocks_total, BLOCK, MODEL_WIDTH).astype(jnp.float32)
    chosen_down = down_weights[adapter_of_block].astype(jnp.float32)
    chosen_up = up_weights[adapter_of_block].astype(jnp.float32)
    positions = jnp.arange(BLOCK, dtype=jnp.int32)
    live_mask = positions[None, :] < block_live_count[:, None]
    grad_blocks = jnp.where(live_mask[:, :, None], cotangent.reshape(blocks_total, BLOCK, QUERY_WIDTH), jnp.zeros((), cotangent.dtype))
    reduced_rank = jnp.einsum("uqv,upv->upq", input_blocks, chosen_down)
    reduced_rounded = reduced_rank.astype(jnp.bfloat16)
    base_output = jnp.dot(tokens, query_weight, preferred_element_type=jnp.float32)
    adapter_output = 2.0 * jnp.einsum("psw,psd->pwd", reduced_rounded.astype(jnp.float32), chosen_up)
    query = (base_output + adapter_output.reshape(TOKEN_SLOTS, QUERY_WIDTH)).astype(jnp.bfloat16)
    grad_rank = 2.0 * jnp.einsum("bkq,brq->brk", grad_blocks.astype(jnp.float32), chosen_up)
    gradient_rounded = grad_rank.astype(jnp.bfloat16)
    group_cols = QUERY_WIDTH // N_TENSOR
    grad_flat = grad_blocks.reshape(TOKEN_SLOTS, QUERY_WIDTH)
    grad_groups = grad_flat.reshape(TOKEN_SLOTS, N_TENSOR, group_cols).transpose(1, 0, 2)
    weight_groups = query_weight.reshape(MODEL_WIDTH, N_TENSOR, group_cols).transpose(1, 0, 2)

    def add_group(total, pair):
        grad_part, weight_part = pair
        product = jnp.dot(grad_part, weight_part.T, preferred_element_type=jnp.float32)
        rounded = lax.optimization_barrier(product.astype(jnp.bfloat16))
        return total + rounded.astype(jnp.float32), None

    summed_output, unused = lax.scan(add_group, jnp.zeros((TOKEN_SLOTS, MODEL_WIDTH), jnp.float32), (grad_groups, weight_groups))
    adapter_backward = jnp.einsum("jxq,jxo->jqo", gradient_rounded.astype(jnp.float32), chosen_down).reshape(TOKEN_SLOTS, MODEL_WIDTH)
    token_gradient = (summed_output + adapter_backward).astype(jnp.bfloat16)
    down_products = jnp.einsum("pgz,pzq->pgq", gradient_rounded.astype(jnp.float32), input_blocks)
    up_terms = 2.0 * jnp.einsum("brk,bkq->brq", reduced_rounded.astype(jnp.float32), grad_blocks.astype(jnp.float32))
    adapter_hits = (adapter_of_block[:, None] == jnp.arange(ADAPTER_COUNT, dtype=jnp.int32)[None, :]).astype(jnp.float32)
    grad_down = jnp.einsum("ba,brd->ard", adapter_hits, down_products, precision=lax.Precision.HIGHEST)
    grad_up = jnp.einsum("ba,brq->arq", adapter_hits, up_terms, precision=lax.Precision.HIGHEST)
    return (query, token_gradient, grad_down, grad_up)
```

```python
import jax
import jax.numpy as jnp
from jax import lax
from jax.sharding import PartitionSpec as P

ADAPTER_COUNT = 32
BLOCK = 128
F32 = jnp.float32
BF16 = jnp.bfloat16


def bit_reversed(index, count):
    result = 0
    while count > 1:
        result = result * 2 + index % 2
        index, count = index // 2, count // 2
    return result


def pick(stacked, index):
    return lax.dynamic_index_in_dim(stacked, index, 0, keepdims=False)


def make_local(n):
    reversed_at = [bit_reversed(q, n) for q in range(n)]
    masks = []
    while 2 ** len(masks) < n:
        masks.append(2 ** len(masks))

    def swap(x, mask):
        return lax.ppermute(x, "tensor", [(t, t ^ mask) for t in range(n)])

    def rotate(x, k):
        return lax.ppermute(x, "dp", [(i, (i + k) % n) for i in range(n)])

    def local(
        tokens,
        query_weight,
        down_weights,
        up_weights,
        cotangent,
        adapter_of_block,
        block_live_count,
    ):
        blocks_here = adapter_of_block.shape[0]
        rows, width = tokens.shape
        columns = query_weight.shape[1]
        group = rows // n
        t = lax.axis_index("tensor")
        i = lax.axis_index("dp")
        place = jnp.array(reversed_at, jnp.int32)

        positions = lax.broadcasted_iota(jnp.int32, (blocks_here, BLOCK), 1)
        live_mask = positions < block_live_count[:, None]
        grad_blocks = jnp.where(
            live_mask[:, :, None],
            cotangent.reshape(blocks_here, BLOCK, columns),
            jnp.zeros((), cotangent.dtype),
        )
        grad_flat = grad_blocks.reshape(rows, columns)

        with jax.named_scope("spread_tokens"):
            grouped = tokens.reshape(n, group, width)
            pieces = [pick(grouped, place[t])]
            for k in range(1, n):
                pieces.append(swap(pick(grouped, place[t ^ k]), k))
            pieces = jnp.stack(pieces)
            by_source = [None] * n
            by_source[0] = pick(pieces, i ^ t)
            for k in sorted(range(1, n), key=lambda k: -abs(2 * k - n)):
                by_source[(n - k) % n] = rotate(pick(pieces, ((i + k) % n) ^ t), k)
            full = [x[None] for x in by_source]
            full = jnp.stack(full)
            for mask in reversed(masks):
                full = jnp.concatenate([full, swap(full, mask)], axis=1)
        order = [0]
        for mask in reversed(masks):
            order = order + [k ^ mask for k in order]

        with jax.named_scope("spread_cotangent"):
            up, down = [grad_flat], [grad_flat]
            for s in range(1, n):
                up.append(lax.ppermute(up[-1], "dp", [(a, a + 1) for a in range(s - 1, n - 1)]))
                down.append(lax.ppermute(down[-1], "dp", [(a + 1, a) for a in range(n - s)]))
            grads = [grad_flat] + [
                jnp.where(i + r <= n - 1, down[r], up[n - r]) for r in range(1, n)
            ]

        with jax.named_scope("ranks"):
            token_blocks = tokens.reshape(blocks_here, BLOCK, width)
            chosen_down = down_weights[adapter_of_block]
            chosen_up = up_weights[adapter_of_block]
            ranks = jnp.stack(
                [
                    jnp.einsum(
                        "uqv,upv->upq", token_blocks, chosen_down, preferred_element_type=F32
                    ),
                    2.0
                    * jnp.einsum("bkq,brq->brk", grad_blocks, chosen_up, preferred_element_type=F32),
                ]
            )
            for mask in masks:
                ranks = ranks + swap(ranks, mask)
            ranks = ranks.astype(BF16)
            shrunk, grad_rank = ranks[0], ranks[1]

        with jax.named_scope("tables"):
            products = jnp.stack(
                [
                    jnp.einsum("pgz,pzq->pgq", grad_rank, token_blocks, preferred_element_type=F32),
                    2.0
                    * jnp.einsum("brk,bkq->brq", shrunk, grad_blocks, preferred_element_type=F32),
                ],
                axis=1,
            ).astype(BF16)
            products = lax.all_gather(products, "dp", axis=0, tiled=True)
            ids = lax.all_gather(adapter_of_block, "dp", axis=0, tiled=True)
            hits = (
                lax.broadcasted_iota(jnp.int32, (ADAPTER_COUNT, ids.shape[0]), 0) == ids[None, :]
            ).astype(BF16)
            grad_down = jnp.einsum("ab,brd->ard", hits, products[:, 0], preferred_element_type=F32)
            grad_up = jnp.einsum("ab,brd->ard", hits, products[:, 1], preferred_element_type=F32)

        with jax.named_scope("forward"):
            parts = []
            for r in range(n):
                parts.append(
                    jnp.dot(
                        full[r].reshape(rows, width), query_weight, preferred_element_type=F32
                    ).astype(BF16)
                )
            up_sum = down_sum = None
            for s in range(1, n):
                d = n - s
                send_up = parts[d] if up_sum is None else parts[d] + up_sum
                send_down = parts[n - d] if down_sum is None else parts[n - d] + down_sum
                up_sum = lax.ppermute(send_up, "dp", [(a, a + 1) for a in range(s)])
                down_sum = lax.ppermute(send_down, "dp", [(a, a - 1) for a in range(d, n)])
            base = parts[0].astype(F32) + up_sum.astype(F32) + down_sum.astype(F32)
            base = base.reshape(n, group, columns)

        position = jnp.array([order.index(k) for k in range(n)], jnp.int32)
        natural = sorted(range(n), key=lambda q: reversed_at[q])

        def in_place(groups):
            return jnp.concatenate(
                [pick(groups, position[q ^ t]) for q in natural], axis=0
            )

        adapter_output = 2.0 * jnp.einsum(
            "psw,psd->pwd", shrunk, chosen_up, preferred_element_type=F32
        )
        query = (in_place(base) + adapter_output.reshape(rows, columns)).astype(BF16)

        with jax.named_scope("backward"):
            sums = [None] * n
            for r in range(n):
                value = lax.dot_general(
                    grads[r], query_weight, (((1,), (1,)), ((), ())), preferred_element_type=F32
                ).astype(BF16)
                for mask in masks:
                    halves = value.reshape(2, value.shape[0] // 2, width)
                    bit = (t // mask) % 2
                    value = pick(halves, bit) + swap(pick(halves, 1 - bit), mask)
                sums[r] = value
            home = [sums[0]] + [rotate(sums[r], r) for r in range(1, n)]
            home = jnp.stack(home)
            back = [pick(home, (i - t) % n)]
            for k in range(1, n):
                back.append(swap(pick(home, (i - (t ^ k)) % n), k))
            back = jnp.stack([back[k] for k in order])
            adapter_backward = jnp.einsum(
                "jxq,jxo->jqo", grad_rank, chosen_down, preferred_element_type=F32
            )
            token_gradient = (
                in_place(back.astype(F32)) + adapter_backward.reshape(rows, width)
            ).astype(BF16)
        return (query, token_gradient, grad_down, grad_up)

    return local


def solution(mesh):
    assert mesh.shape["dp"] == mesh.shape["tensor"]
    return jax.shard_map(
        make_local(mesh.shape["tensor"]),
        mesh=mesh,
        in_specs=(
            P(("parts", "dp"), "tensor"),
            P("dp", "tensor"),
            P("parts", None, "tensor"),
            P("parts", None, "tensor"),
            P(("parts", "dp"), "tensor"),
            P(("parts", "dp")),
            P(("parts", "dp")),
        ),
        out_specs=(
            P(("parts", "dp"), "tensor"),
            P(("parts", "dp"), "tensor"),
            P("parts", None, "tensor"),
            P("parts", None, "tensor"),
        ),
        check_vma=False,
    )
```

```python
import jax
import jax.numpy as jnp
from jax import lax
from jax.sharding import PartitionSpec as P

ADAPTER_COUNT = 32
BLOCK = 128
F32 = jnp.float32
BF16 = jnp.bfloat16


def bit_reversed(index, count):
    result = 0
    while count > 1:
        result = result * 2 + index % 2
        index, count = index // 2, count // 2
    return result


def pick(stacked, index):
    return lax.dynamic_index_in_dim(stacked, index, 0, keepdims=False)


def make_local(n):
    reversed_at = [bit_reversed(q, n) for q in range(n)]
    masks = []
    while 2 ** len(masks) < n:
        masks.append(2 ** len(masks))

    def swap(x, mask):
        return lax.ppermute(x, "tensor", [(t, t ^ mask) for t in range(n)])

    def rotate(x, k):
        return lax.ppermute(x, "dp", [(i, (i + k) % n) for i in range(n)])

    def local(
        tokens,
        query_weight,
        down_weights,
        up_weights,
        cotangent,
        adapter_of_block,
        block_live_count,
    ):
        blocks_here = adapter_of_block.shape[0]
        rows, width = tokens.shape
        columns = query_weight.shape[1]
        group = rows // n
        t = lax.axis_index("tensor")
        i = lax.axis_index("dp")
        positions = lax.broadcasted_iota(jnp.int32, (blocks_here, BLOCK), 1)
        live_mask = positions < block_live_count[:, None]
        grad_blocks = jnp.where(
            live_mask[:, :, None],
            cotangent.reshape(blocks_here, BLOCK, columns),
            jnp.zeros((), cotangent.dtype),
        )
        grad_flat = grad_blocks.reshape(rows, columns)

        with jax.named_scope("spread_tokens"):
            pieces = lax.all_to_all(
                jnp.stack([tokens[group * p : group * (p + 1)] for p in reversed_at]),
                "tensor",
                0,
                0,
            )
            by_source = {0: pick(pieces, i)}
            distances = sorted(range(1, n), key=lambda k: -abs(2 * k - n))
            for k in distances:
                by_source[n - k] = rotate(pick(pieces, (i + k) % n), k)
            near = [n - k for k in distances if k in (1, n - 1)]
            rest = [r for r in range(n) if r not in near]
            full = {}
            for batch in (near, rest):
                held = jnp.stack([by_source[r] for r in batch])[:, None]
                for mask in reversed(masks):
                    held = jnp.concatenate([held, swap(held, mask)], axis=1)
                for at, r in enumerate(batch):
                    full[r] = held[at].reshape(rows, width)
                last_held = held
        order = [0]
        for mask in reversed(masks):
            order = order + [k ^ mask for k in order]

        with jax.named_scope("spread_cotangent"):
            up, down = [grad_flat], [grad_flat]
            for s in range(1, n):
                up.append(lax.ppermute(up[-1], "dp", [(a, a + 1) for a in range(s - 1, n - 1)]))
                down.append(lax.ppermute(down[-1], "dp", [(a + 1, a) for a in range(n - s)]))
                if s == 1:
                    up[1], down[1], _ = lax.optimization_barrier(
                        (up[1], down[1], by_source[n // 2])
                    )
            grads = [grad_flat] + [
                jnp.where(i + r <= n - 1, down[r], up[n - r]) for r in range(1, n)
            ]

        with jax.named_scope("ranks"):
            token_blocks = tokens.reshape(blocks_here, BLOCK, width)
            chosen_down = down_weights[adapter_of_block]
            chosen_up = up_weights[adapter_of_block]
            ranks = jnp.stack(
                [
                    jnp.einsum(
                        "uqv,upv->upq", token_blocks, chosen_down, preferred_element_type=F32
                    ),
                    2.0
                    * jnp.einsum("bkq,brq->brk", grad_blocks, chosen_up, preferred_element_type=F32),
                ]
            )
            for mask in masks:
                ranks = ranks + swap(ranks, mask)
            ranks = ranks.astype(BF16)
            shrunk, grad_rank = ranks[0], ranks[1]

        with jax.named_scope("tables"):
            ids = jnp.broadcast_to(
                adapter_of_block[:, None, None].astype(BF16), (blocks_here, 1, width)
            )
            products = jnp.concatenate(
                [
                    jnp.einsum(
                        "pgz,pzq->pgq", grad_rank, token_blocks, preferred_element_type=F32
                    ).astype(BF16),
                    (
                        2.0
                        * jnp.einsum(
                            "brk,bkq->brq", shrunk, grad_blocks, preferred_element_type=F32
                        )
                    ).astype(BF16),
                    ids,
                ],
                axis=1,
            )
            products = lax.all_gather(products, "dp", axis=0, tiled=True)
            rank = shrunk.shape[1]
            ids = products[:, 2 * rank, 0].astype(jnp.int32)
            hits = (
                lax.broadcasted_iota(jnp.int32, (ADAPTER_COUNT, ids.shape[0]), 0) == ids[None, :]
            ).astype(BF16)
            grad_down = jnp.einsum(
                "ab,brd->ard", hits, products[:, :rank], preferred_element_type=F32
            )
            grad_up = jnp.einsum(
                "ab,brd->ard", hits, products[:, rank : 2 * rank], preferred_element_type=F32
            )

        with jax.named_scope("forward"):
            parts = {
                r: jnp.dot(full[r], query_weight, preferred_element_type=F32).astype(BF16)
                for r in range(1, n)
            }
            up_sum = down_sum = None
            for s in range(1, n):
                d = n - s
                send_up = parts[d] if up_sum is None else parts[d] + up_sum
                send_down = parts[n - d] if down_sum is None else parts[n - d] + down_sum
                up_sum = lax.ppermute(send_up, "dp", [(a, a + 1) for a in range(s)])
                down_sum = lax.ppermute(send_down, "dp", [(a, a - 1) for a in range(d, n)])
            own = jnp.dot(full[0], query_weight, preferred_element_type=F32)
            base = own + up_sum.astype(F32) + down_sum.astype(F32)
            base = base.reshape(n, group, columns)

        position = jnp.array([order.index(k) for k in range(n)], jnp.int32)
        natural = sorted(range(n), key=lambda q: reversed_at[q])

        def in_place(groups):
            return jnp.concatenate([pick(groups, position[q ^ t]) for q in natural], axis=0)

        adapter_output = 2.0 * jnp.einsum(
            "psw,psd->pwd", shrunk, chosen_up, preferred_element_type=F32
        )
        query = (in_place(base) + adapter_output.reshape(rows, columns)).astype(BF16)

        with jax.named_scope("backward"):
            early = [r for r in range(n) if r in (0, n // 2)]
            late = [r for r in range(n) if r not in early]
            sums = {}
            for batch in (early, late):
                held = jnp.stack([grads[r] for r in batch]).reshape(-1, columns)
                if batch is early:
                    held, _ = lax.optimization_barrier((held, last_held))
                value = (
                    lax.dot_general(
                        held, query_weight, (((1,), (1,)), ((), ())), preferred_element_type=F32
                    )
                    .astype(BF16)
                    .reshape(len(batch), rows, width)
                )
                for mask in masks:
                    halves = value.reshape(len(batch), 2, value.shape[1] // 2, width)
                    bit = (t // mask) % 2
                    value = lax.dynamic_index_in_dim(halves, bit, 1, keepdims=False) + swap(
                        lax.dynamic_index_in_dim(halves, 1 - bit, 1, keepdims=False), mask
                    )
                for at, r in enumerate(batch):
                    sums[r] = value[at]
            sums = jnp.stack([sums[r] for r in range(n)])
            back = []
            for m in range(n):
                back.append(
                    lax.ppermute(
                        pick(sums, (t + m) % n),
                        ("dp", "tensor"),
                        [
                            (a * n + b, ((a + b + m) % n) * n + a)
                            for a in range(n)
                            for b in range(n)
                        ],
                    )
                )
            back = jnp.stack(back).astype(F32)
            returned = jnp.concatenate([pick(back, (i - t - q) % n) for q in natural], axis=0)
            adapter_backward = jnp.einsum(
                "jxq,jxo->jqo", grad_rank, chosen_down, preferred_element_type=F32
            )
            token_gradient = (returned + adapter_backward.reshape(rows, width)).astype(BF16)
        return (query, token_gradient, grad_down, grad_up)

    return local


def solution(mesh):
    assert mesh.shape["dp"] == mesh.shape["tensor"]
    return jax.shard_map(
        make_local(mesh.shape["tensor"]),
        mesh=mesh,
        in_specs=(
            P(("parts", "dp"), "tensor"),
            P("dp", "tensor"),
            P("parts", None, "tensor"),
            P("parts", None, "tensor"),
            P(("parts", "dp"), "tensor"),
            P(("parts", "dp")),
            P(("parts", "dp")),
        ),
        out_specs=(
            P(("parts", "dp"), "tensor"),
            P(("parts", "dp"), "tensor"),
            P("parts", None, "tensor"),
            P("parts", None, "tensor"),
        ),
        check_vma=False,
    )
```

```python
import jax
import jax.numpy as jnp
from jax import lax
from jax.sharding import PartitionSpec as P

ADAPTER_COUNT = 32
BLOCK = 128
F32 = jnp.float32
BF16 = jnp.bfloat16


def pick(stacked, index):
    return lax.dynamic_index_in_dim(stacked, index, 0, keepdims=False)


def after(values, *earlier):
    return lax.optimization_barrier((tuple(values), earlier))[0]


def make_local(n):
    masks = []
    while 2 ** len(masks) < n:
        masks.append(2 ** len(masks))

    def swap(x, mask):
        return lax.ppermute(x, "tensor", [(t, t ^ mask) for t in range(n)])

    def rotate(x, k):
        return lax.ppermute(x, "dp", [(i, (i + k) % n) for i in range(n)])

    def local(
        tokens,
        query_weight,
        down_weights,
        up_weights,
        cotangent,
        adapter_of_block,
        block_live_count,
    ):
        blocks_here = adapter_of_block.shape[0]
        rows, width = tokens.shape
        columns = query_weight.shape[1]
        rank = down_weights.shape[1]
        group = rows // n
        t = lax.axis_index("tensor")
        i = lax.axis_index("dp")

        positions = lax.broadcasted_iota(jnp.int32, (blocks_here, BLOCK), 1)
        live_mask = positions < block_live_count[:, None]
        grad_blocks = jnp.where(
            live_mask[:, :, None],
            cotangent.reshape(blocks_here, BLOCK, columns),
            jnp.zeros((), cotangent.dtype),
        )
        grad_flat = grad_blocks.reshape(rows, columns)

        def hop(s, rising, falling):
            with jax.named_scope("spread_cotangent"):
                return (
                    lax.ppermute(rising, "dp", [(a, a + 1) for a in range(s - 1, n - 1)]),
                    lax.ppermute(falling, "dp", [(a + 1, a) for a in range(n - s)]),
                )

        up, down = {}, {}
        up[1], down[1] = hop(1, grad_flat, grad_flat)

        with jax.named_scope("spread_tokens"):
            pieces = lax.all_to_all(
                tokens.reshape(n, group, width), "tensor", 0, 0
            )
            distances = sorted(range(1, n), key=lambda k: -abs(2 * k - n))
            by_source = {0: pick(pieces, i)}
            for k in distances:
                by_source[n - k] = rotate(pick(pieces, (i + k) % n), k)
            near = [n - k for k in distances if k in (1, n - 1)]
            rest = [r for r in range(n) if r not in near]
            full = {}
            for batch in (near, rest):
                held = jnp.stack([by_source[r] for r in batch])
                if batch is near:
                    held, up[1], down[1] = after((held, up[1], down[1]))
                for at, mask in enumerate(reversed(masks)):
                    other = swap(held, mask)
                    odd = (t // mask) % 2 == 1
                    held = jnp.stack(
                        [jnp.where(odd, other, held), jnp.where(odd, held, other)], axis=1 + at
                    )
                for at, r in enumerate(batch):
                    full[r] = held[at].reshape(rows, width)

        with jax.named_scope("ranks"):
            token_blocks = tokens.reshape(blocks_here, BLOCK, width)
            chosen_down = down_weights[adapter_of_block]
            chosen_up = up_weights[adapter_of_block]
            ranks = jnp.stack(
                [
                    jnp.einsum(
                        "uqv,upv->upq", token_blocks, chosen_down, preferred_element_type=F32
                    ),
                    2.0
                    * jnp.einsum("bkq,brq->brk", grad_blocks, chosen_up, preferred_element_type=F32),
                ]
            )
            for mask in masks:
                ranks = ranks + swap(ranks, mask)
            ranks = ranks.astype(BF16)
            shrunk, grad_rank = ranks[0], ranks[1]
            adapter_output = 2.0 * jnp.einsum(
                "psw,psd->pwd", shrunk, chosen_up, preferred_element_type=F32
            ).reshape(rows, columns)
            adapter_backward = jnp.einsum(
                "jxq,jxo->jqo", grad_rank, chosen_down, preferred_element_type=F32
            ).reshape(rows, width)
            (adapter_backward,) = after((adapter_backward,))

        with jax.named_scope("tables"):
            down_products = jnp.einsum(
                "pgz,pzq->pgq", grad_rank, token_blocks, preferred_element_type=F32
            ).astype(BF16)
            ids = jnp.broadcast_to(
                adapter_of_block[:, None, None].astype(BF16), (blocks_here, 1, width)
            )
            parcel = jnp.concatenate(
                [down_products, ids, shrunk.reshape(blocks_here, -1, width)], axis=1
            )
            (parcel,) = after((parcel,), *[by_source[r] for r in range(n)])
            parcel = lax.all_gather(parcel, "dp", axis=0, tiled=True)
            blocks = parcel.shape[0]
            ids = parcel[:, rank, 0].astype(jnp.int32)
            all_shrunk = parcel[:, rank + 1 :].reshape(n, blocks_here, rank, BLOCK)
            shape = (ADAPTER_COUNT, rank, blocks, rank)
            hits = (
                (lax.broadcasted_iota(jnp.int32, shape, 0) == ids[None, None, :, None])
                & (
                    lax.broadcasted_iota(jnp.int32, shape, 1)
                    == lax.broadcasted_iota(jnp.int32, shape, 3)
                )
            ).astype(BF16)
            hits = hits.reshape(ADAPTER_COUNT * rank, blocks * rank)

            def table(products):
                return jnp.dot(
                    hits,
                    products.reshape(blocks * rank, products.shape[-1]),
                    preferred_element_type=F32,
                ).reshape(ADAPTER_COUNT, rank, products.shape[-1])

            grad_down = table(parcel[:, :rank])

        with jax.named_scope("forward"):

            def project(r):
                return jnp.dot(full[r], query_weight, preferred_element_type=F32)

            parts = dict(zip(near, after([project(r).astype(BF16) for r in near])))
            near_parts = tuple(parts.values())
            for r in rest:
                if r != 0:
                    (parts[r],) = after((project(r).astype(BF16),), *near_parts)
            (own,) = after((project(0) + adapter_output,), *near_parts)
            up_sum = down_sum = None
            sends = {}
            for s in range(1, n):
                d = n - s
                sends[s] = (
                    (parts[d], parts[n - d])
                    if s == 1
                    else (parts[d] + up_sum, parts[n - d] + down_sum)
                )
                up_sum = lax.ppermute(sends[s][0], "dp", [(a, a + 1) for a in range(s)])
                down_sum = lax.ppermute(sends[s][1], "dp", [(a, a - 1) for a in range(d, n)])
            query = (own + up_sum.astype(F32) + down_sum.astype(F32)).astype(BF16)

        for s in range(2, n):
            up[s - 1], down[s - 1] = after((up[s - 1], down[s - 1]), *sends[s - 1])
            up[s], down[s] = hop(s, up[s - 1], down[s - 1])
        up[n - 1], down[n - 1] = after((up[n - 1], down[n - 1]), *sends[n - 1])
        grads = [grad_flat] + [jnp.where(i + r <= n - 1, down[r], up[n - r]) for r in range(1, n)]

        with jax.named_scope("backward"):
            early = [r for r in range(n) if r in (0, n // 2)]
            late = [r for r in range(n) if r not in early]
            sums = {}
            up_products = {}
            for batch in (early, late):
                held = [grads[r] for r in batch]
                if batch is early:
                    held = after(held, own, *parts.values())
                held = jnp.stack(held)
                value = (
                    lax.dot_general(
                        held.reshape(-1, columns),
                        query_weight,
                        (((1,), (1,)), ((), ())),
                        preferred_element_type=F32,
                    )
                    .astype(BF16)
                    .reshape(len(batch), n, group, width)
                )
                for mask in masks:
                    halves = value.reshape(len(batch), value.shape[1] // 2, 2, group, width)
                    bit = (t // mask) % 2
                    value = lax.dynamic_index_in_dim(halves, bit, 2, keepdims=False) + swap(
                        lax.dynamic_index_in_dim(halves, 1 - bit, 2, keepdims=False), mask
                    )
                for at, r in enumerate(batch):
                    sums[r] = value[at, 0]
                with jax.named_scope("tables"):
                    for at, r in enumerate(batch):
                        up_products[r] = (
                            2.0
                            * jnp.einsum(
                                "brk,bkq->brq",
                                pick(all_shrunk, (i + r) % n),
                                held[at].reshape(blocks_here, BLOCK, columns),
                                preferred_element_type=F32,
                            )
                        ).astype(BF16)
            sums = jnp.stack([sums[r] for r in range(n)])
            back = [
                lax.ppermute(
                    pick(sums, (t + m) % n),
                    ("dp", "tensor"),
                    [(a * n + b, ((a + b + m) % n) * n + a) for a in range(n) for b in range(n)],
                )
                for m in range(n)
            ]
            returned = jnp.concatenate(
                [lax.select_n((i - t - q) % n, *back) for q in range(n)], axis=0
            )
            token_gradient = (returned.astype(F32) + adapter_backward).astype(BF16)

        with jax.named_scope("tables"):
            up_products = jnp.stack([up_products[r] for r in range(n)])
            grad_up = table(
                jnp.concatenate([pick(up_products, (g - i) % n) for g in range(n)], axis=0)
            )
        return (query, token_gradient, grad_down, grad_up)

    return local


def solution(mesh):
    assert mesh.shape["dp"] == mesh.shape["tensor"]
    return jax.shard_map(
        make_local(mesh.shape["tensor"]),
        mesh=mesh,
        in_specs=(
            P(("parts", "dp"), "tensor"),
            P("dp", "tensor"),
            P("parts", None, "tensor"),
            P("parts", None, "tensor"),
            P(("parts", "dp"), "tensor"),
            P(("parts", "dp")),
            P(("parts", "dp")),
        ),
        out_specs=(
            P(("parts", "dp"), "tensor"),
            P(("parts", "dp"), "tensor"),
            P("parts", None, "tensor"),
            P("parts", None, "tensor"),
        ),
        check_vma=False,
    )
```

```python
import jax
import jax.numpy as jnp
from jax import lax
from jax.sharding import PartitionSpec as P

ADAPTER_COUNT = 32
BLOCK = 128
F32 = jnp.float32
BF16 = jnp.bfloat16


def pick(stacked, index):
    return lax.dynamic_index_in_dim(stacked, index, 0, keepdims=False)


def after(values, *earlier):
    return lax.optimization_barrier((tuple(values), earlier))[0]


def make_local(n):
    masks = []
    while 2 ** len(masks) < n:
        masks.append(2 ** len(masks))

    def swap(x, mask):
        return lax.ppermute(x, "tensor", [(t, t ^ mask) for t in range(n)])

    def rotate(x, k):
        return lax.ppermute(x, "dp", [(i, (i + k) % n) for i in range(n)])

    def local(
        tokens,
        query_weight,
        down_weights,
        up_weights,
        cotangent,
        adapter_of_block,
        block_live_count,
    ):
        blocks_here = adapter_of_block.shape[0]
        rows, width = tokens.shape
        columns = query_weight.shape[1]
        rank = down_weights.shape[1]
        group = rows // n
        t = lax.axis_index("tensor")
        i = lax.axis_index("dp")
        half = n // 2
        lower = i < half

        positions = lax.broadcasted_iota(jnp.int32, (blocks_here, BLOCK), 1)
        live_mask = positions < block_live_count[:, None]
        grad_blocks = jnp.where(
            live_mask[:, :, None],
            cotangent.reshape(blocks_here, BLOCK, columns),
            jnp.zeros((), cotangent.dtype),
        )
        grad_flat = grad_blocks.reshape(rows, columns)

        def hop(s, rising, falling):
            with jax.named_scope("spread_cotangent"):
                return (
                    lax.ppermute(rising, "dp", [(a, a + 1) for a in range(s - 1, n - 1)]),
                    lax.ppermute(falling, "dp", [(a + 1, a) for a in range(n - s)]),
                )

        with jax.named_scope("spread_tokens"):
            pieces = lax.all_to_all(
                tokens.reshape(n, group, width), "tensor", 0, 0
            )

        with jax.named_scope("ranks"):
            token_blocks = tokens.reshape(blocks_here, BLOCK, width)
            chosen_down = down_weights[adapter_of_block]
            chosen_up = up_weights[adapter_of_block]
            ranks = jnp.stack(
                [
                    jnp.einsum(
                        "uqv,upv->upq", token_blocks, chosen_down, preferred_element_type=F32
                    ),
                    2.0
                    * jnp.einsum("bkq,brq->brk", grad_blocks, chosen_up, preferred_element_type=F32),
                ]
            )
            for mask in masks:
                ranks = ranks + swap(ranks, mask)
            ranks = ranks.astype(BF16)
            shrunk, grad_rank = ranks[0], ranks[1]
            adapter_output = 2.0 * jnp.einsum(
                "psw,psd->pwd", shrunk, chosen_up, preferred_element_type=F32
            ).reshape(rows, columns)
            adapter_backward = jnp.einsum(
                "jxq,jxo->jqo", grad_rank, chosen_down, preferred_element_type=F32
            ).reshape(rows, width)
            (adapter_backward,) = after((adapter_backward,))

        with jax.named_scope("tables"):
            down_products = jnp.einsum(
                "pgz,pzq->pgq", grad_rank, token_blocks, preferred_element_type=F32
            ).astype(BF16)
            ids = jnp.broadcast_to(
                adapter_of_block[:, None, None].astype(BF16), (blocks_here, 1, width)
            )
            parcel = jnp.concatenate(
                [down_products, ids, shrunk.reshape(blocks_here, -1, width)], axis=1
            )

        spare = -blocks_here * parcel.shape[1] % 16
        load = jnp.concatenate(
            [
                grad_flat,
                parcel.reshape(-1, width),
                jnp.zeros((spare, width), BF16),
            ]
        )
        up, down = {}, {}
        up[1], down[1] = hop(1, load, load)

        with jax.named_scope("spread_tokens"):
            distances = sorted(range(1, n), key=lambda k: -abs(2 * k - n))
            by_source = {0: pick(pieces, i)}
            for k in distances:
                by_source[n - k] = rotate(pick(pieces, (i + k) % n), k)
            near = [n - k for k in distances if k in (1, n - 1)]
            rest = [r for r in range(n) if r not in near]
            full = {}
            for batch in (near, rest):
                held = jnp.stack([by_source[r] for r in batch])
                for at, mask in enumerate(reversed(masks)):
                    other = swap(held, mask)
                    odd = (t // mask) % 2 == 1
                    held = jnp.stack(
                        [jnp.where(odd, other, held), jnp.where(odd, held, other)], axis=1 + at
                    )
                for at, r in enumerate(batch):
                    full[r] = held[at].reshape(rows, width)

        with jax.named_scope("forward"):

            def project(r):
                return jnp.dot(full[r], query_weight, preferred_element_type=F32)

            parts = dict(zip(near, after([project(r).astype(BF16) for r in near])))
            near_parts = tuple(parts.values())
            for r in rest:
                if r != 0:
                    (parts[r],) = after((project(r).astype(BF16),), *near_parts)
            (own,) = after((project(0) + adapter_output,), *near_parts)

        def pull_back(batch):
            return lax.dot_general(
                jnp.concatenate([value[:rows] for value in batch]),
                query_weight,
                (((1,), (1,)), ((), ())),
                preferred_element_type=F32,
            ).astype(BF16)

        def halve(value, masks_here):
            for mask in masks_here:
                count = value.shape[0]
                halves = value.reshape(count, value.shape[1] // 2, 2, group, width)
                bit = (t // mask) % 2
                value = lax.dynamic_index_in_dim(halves, bit, 2, keepdims=False) + swap(
                    lax.dynamic_index_in_dim(halves, 1 - bit, 2, keepdims=False), mask
                )
            return value

        up_sum = down_sum = None
        for s in range(1, n):
            d = n - s
            with jax.named_scope("forward"):
                sends = (
                    (parts[d], parts[n - d])
                    if s == 1
                    else (parts[d] + up_sum, parts[n - d] + down_sum)
                )
                if s == 2:
                    first = after([load, jnp.where(lower, down[1], up[1])], own)
                    first_value = pull_back(first).reshape(-1, n, group, width)
                    *sends, first_value = after((*sends, first_value))
                    first_value = halve(first_value, masks)[:, 0]
                if s == n - 1:
                    middle = after(
                        [jnp.where(lower, down[r], up[r]) for r in range(2, half + 1)], own
                    )
                    middle_value = pull_back(middle).reshape(-1, n, group, width)
                    *sends, middle_value = after((*sends, middle_value))
                up_sum = lax.ppermute(sends[0], "dp", [(a, a + 1) for a in range(s)])
                down_sum = lax.ppermute(sends[1], "dp", [(a, a - 1) for a in range(d, n)])
            up[s], down[s] = after((up[s], down[s]), *(near_parts if s == 1 else sends))
            if s < n - 1:
                up[s + 1], down[s + 1] = hop(s + 1, up[s], down[s])
        with jax.named_scope("forward"):
            query = (own + up_sum.astype(F32) + down_sum.astype(F32)).astype(BF16)

        def slot(r):
            k = jnp.minimum(r, n - r)
            return jnp.where((r == 0) | (r == half), r, jnp.where((r < half) == lower, k, half + k))

        def distance(at):
            if at <= half:
                return jnp.where(lower, at, (n - at) % n)
            return jnp.where(lower, n + half - at, at - half)

        late = [
            jnp.where(
                lower,
                jnp.where(i >= r, up[r], down[n - r]),
                jnp.where(i + r <= n - 1, down[r], up[n - r]),
            )
            for r in range(1, half)
        ]
        loads = [*first, *middle, *late]

        with jax.named_scope("backward"):
            late_value = pull_back(late).reshape(-1, n, group, width)
            last_value = halve(jnp.concatenate([middle_value, late_value]), masks)[:, 0]
            sums = jnp.concatenate([first_value, last_value])
            back = [
                lax.ppermute(
                    pick(sums, slot((t + m) % n)),
                    ("dp", "tensor"),
                    [(a * n + b, ((a + b + m) % n) * n + a) for a in range(n) for b in range(n)],
                )
                for m in range(n)
            ]
            returned = jnp.concatenate(
                [lax.select_n((i - t - q) % n, *back) for q in range(n)], axis=0
            )
            token_gradient = (returned.astype(F32) + adapter_backward).astype(BF16)

        with jax.named_scope("tables"):
            *loads, sums = after((*loads, sums))
            grads = [value[:rows] for value in loads]
            parcels = [
                value[rows : value.shape[0] - spare].reshape(blocks_here, -1, width) for value in loads
            ]
            parcels = jnp.stack(parcels)
            parcel = jnp.concatenate([pick(parcels, slot((g - i) % n)) for g in range(n)], axis=0)
            blocks = parcel.shape[0]
            ids = parcel[:, rank, 0].astype(jnp.int32)
            all_shrunk = parcel[:, rank + 1 :].reshape(n, blocks_here, rank, BLOCK)
            shape = (ADAPTER_COUNT, rank, blocks, rank)
            hits = (
                (lax.broadcasted_iota(jnp.int32, shape, 0) == ids[None, None, :, None])
                & (
                    lax.broadcasted_iota(jnp.int32, shape, 1)
                    == lax.broadcasted_iota(jnp.int32, shape, 3)
                )
            ).astype(BF16)
            hits = hits.reshape(ADAPTER_COUNT * rank, blocks * rank)

            def table(products):
                return jnp.dot(
                    hits,
                    products.reshape(blocks * rank, products.shape[-1]),
                    preferred_element_type=F32,
                ).reshape(ADAPTER_COUNT, rank, products.shape[-1])

            grad_down = table(parcel[:, :rank])
            up_products = jnp.stack(
                [
                    (
                        2.0
                        * jnp.einsum(
                            "brk,bkq->brq",
                            pick(all_shrunk, (i + distance(at)) % n),
                            held.reshape(blocks_here, BLOCK, columns),
                            preferred_element_type=F32,
                        )
                    ).astype(BF16)
                    for at, held in enumerate(grads)
                ]
            )
            grad_up = table(
                jnp.concatenate([pick(up_products, slot((g - i) % n)) for g in range(n)], axis=0)
            )
        return (query, token_gradient, grad_down, grad_up)

    return local


def solution(mesh):
    assert mesh.shape["dp"] == mesh.shape["tensor"]
    return jax.shard_map(
        make_local(mesh.shape["tensor"]),
        mesh=mesh,
        in_specs=(
            P(("parts", "dp"), "tensor"),
            P("dp", "tensor"),
            P("parts", None, "tensor"),
            P("parts", None, "tensor"),
            P(("parts", "dp"), "tensor"),
            P(("parts", "dp")),
            P(("parts", "dp")),
        ),
        out_specs=(
            P(("parts", "dp"), "tensor"),
            P(("parts", "dp"), "tensor"),
            P("parts", None, "tensor"),
            P("parts", None, "tensor"),
        ),
        check_vma=False,
    )
```

```python
import jax
import jax.numpy as jnp
from jax import lax
from jax.sharding import PartitionSpec as P

ADAPTER_COUNT = 32
BLOCK = 128
F32 = jnp.float32
BF16 = jnp.bfloat16


def pick(stacked, index):
    return lax.dynamic_index_in_dim(stacked, index, 0, keepdims=False)


def after(values, *earlier):
    return lax.optimization_barrier((tuple(values), earlier))[0]


def make_local(n):
    masks = []
    while 2 ** len(masks) < n:
        masks.append(2 ** len(masks))

    def swap(x, mask):
        return lax.ppermute(x, "tensor", [(t, t ^ mask) for t in range(n)])

    def rotate(x, k):
        return lax.ppermute(x, "dp", [(i, (i + k) % n) for i in range(n)])

    def local(
        tokens,
        query_weight,
        down_weights,
        up_weights,
        cotangent,
        adapter_of_block,
        block_live_count,
    ):
        blocks_here = adapter_of_block.shape[0]
        rows, width = tokens.shape
        columns = query_weight.shape[1]
        rank = down_weights.shape[1]
        group = rows // n
        t = lax.axis_index("tensor")
        i = lax.axis_index("dp")
        half = n // 2
        lower = i < half

        positions = lax.broadcasted_iota(jnp.int32, (blocks_here, BLOCK), 1)
        live_mask = positions < block_live_count[:, None]
        grad_blocks = jnp.where(
            live_mask[:, :, None],
            cotangent.reshape(blocks_here, BLOCK, columns),
            jnp.zeros((), cotangent.dtype),
        )
        grad_flat = grad_blocks.reshape(rows, columns)

        def hop(s, rising, falling):
            with jax.named_scope("spread_cotangent"):
                return (
                    lax.ppermute(rising, "dp", [(a, a + 1) for a in range(s - 1, n - 1)]),
                    lax.ppermute(falling, "dp", [(a + 1, a) for a in range(n - s)]),
                )

        with jax.named_scope("spread_tokens"):
            pieces = lax.all_to_all(
                tokens.reshape(n, group, width), "tensor", 0, 0
            )

        with jax.named_scope("ranks"):
            token_blocks = tokens.reshape(blocks_here, BLOCK, width)
            chosen_down = down_weights[adapter_of_block]
            chosen_up = up_weights[adapter_of_block]
            ranks = jnp.stack(
                [
                    jnp.einsum(
                        "uqv,upv->upq", token_blocks, chosen_down, preferred_element_type=F32
                    ),
                    2.0
                    * jnp.einsum("bkq,brq->brk", grad_blocks, chosen_up, preferred_element_type=F32),
                ]
            )
            for mask in masks:
                ranks = ranks + swap(ranks, mask)
            ranks = ranks.astype(BF16)
            shrunk, grad_rank = ranks[0], ranks[1]
            adapter_output = 2.0 * jnp.einsum(
                "psw,psd->pwd", shrunk, chosen_up, preferred_element_type=F32
            ).reshape(rows, columns)
            adapter_backward = jnp.einsum(
                "jxq,jxo->jqo", grad_rank, chosen_down, preferred_element_type=F32
            ).reshape(rows, width)
            (adapter_backward,) = after((adapter_backward,))

        with jax.named_scope("tables"):
            down_products = jnp.einsum(
                "pgz,pzq->pgq", grad_rank, token_blocks, preferred_element_type=F32
            ).astype(BF16)
            ids = jnp.broadcast_to(
                adapter_of_block[:, None, None].astype(BF16), (blocks_here, 1, width)
            )
            parcel = jnp.concatenate(
                [down_products, ids, shrunk.reshape(blocks_here, -1, width)], axis=1
            )

        spare = -blocks_here * parcel.shape[1] % 16
        load = jnp.concatenate(
            [
                grad_flat,
                parcel.reshape(-1, width),
                jnp.zeros((spare, width), BF16),
            ]
        )
        up, down = {}, {}
        up[1], down[1] = hop(1, load, load)

        with jax.named_scope("spread_tokens"):
            distances = sorted(range(1, n), key=lambda k: -abs(2 * k - n))
            by_source = {0: pick(pieces, i)}
            for k in distances:
                by_source[n - k] = rotate(pick(pieces, (i + k) % n), k)
            near = [n - k for k in distances if k in (1, n - 1)]
            rest = [r for r in range(n) if r not in near]
            full = {}
            for batch in (near, rest):
                held = jnp.stack([by_source[r] for r in batch])
                for at, mask in enumerate(reversed(masks)):
                    other = swap(held, mask)
                    odd = (t // mask) % 2 == 1
                    held = jnp.stack(
                        [jnp.where(odd, other, held), jnp.where(odd, held, other)], axis=1 + at
                    )
                for at, r in enumerate(batch):
                    full[r] = held[at].reshape(rows, width)

        with jax.named_scope("forward"):

            def project(r):
                return jnp.dot(full[r], query_weight, preferred_element_type=F32)

            parts = dict(zip(near, after([project(r).astype(BF16) for r in near])))
            near_parts = tuple(parts.values())
            for r in rest:
                if r != 0:
                    (parts[r],) = after((project(r).astype(BF16),), *near_parts)
            (own,) = after((project(0) + adapter_output,), *near_parts)

        def pull_back(batch):
            return lax.dot_general(
                jnp.concatenate([value[:rows] for value in batch]),
                query_weight,
                (((1,), (1,)), ((), ())),
                preferred_element_type=F32,
            ).astype(BF16)

        def halve(value, masks_here):
            for mask in masks_here:
                count = value.shape[0]
                halves = value.reshape(count, value.shape[1] // 2, 2, group, width)
                bit = (t // mask) % 2
                value = lax.dynamic_index_in_dim(halves, bit, 2, keepdims=False) + swap(
                    lax.dynamic_index_in_dim(halves, 1 - bit, 2, keepdims=False), mask
                )
            return value

        up_sum = down_sum = None
        for s in range(1, n):
            d = n - s
            with jax.named_scope("forward"):
                sends = (
                    (parts[d], parts[n - d])
                    if s == 1
                    else (parts[d] + up_sum, parts[n - d] + down_sum)
                )
                if s == 2:
                    first = after([load, jnp.where(lower, down[1], up[1])], own)
                    first_value = pull_back(first).reshape(-1, n, group, width)
                    *sends, first_value = after((*sends, first_value))
                    first_value = halve(first_value, masks)[:, 0]
                if s == n - 1:
                    middle = after(
                        [jnp.where(lower, down[r], up[r]) for r in range(2, half + 1)], own
                    )
                    middle_value = pull_back(middle).reshape(-1, n, group, width)
                    *sends, middle_value = after((*sends, middle_value))
                up_sum = lax.ppermute(sends[0], "dp", [(a, a + 1) for a in range(s)])
                down_sum = lax.ppermute(sends[1], "dp", [(a, a - 1) for a in range(d, n)])
            up[s], down[s] = after((up[s], down[s]), *(near_parts if s == 1 else sends))
            if s < n - 1:
                up[s + 1], down[s + 1] = hop(s + 1, up[s], down[s])
        with jax.named_scope("forward"):
            query = (own + up_sum.astype(F32) + down_sum.astype(F32)).astype(BF16)

        def slot(r):
            k = jnp.minimum(r, n - r)
            return jnp.where((r == 0) | (r == half), r, jnp.where((r < half) == lower, k, half + k))

        def distance(at):
            if at <= half:
                return jnp.where(lower, at, (n - at) % n)
            return jnp.where(lower, n + half - at, at - half)

        late = [
            jnp.where(
                lower,
                jnp.where(i >= r, up[r], down[n - r]),
                jnp.where(i + r <= n - 1, down[r], up[n - r]),
            )
            for r in range(1, half)
        ]
        loads = [*first, *middle, *late]

        with jax.named_scope("backward"):
            late_value = pull_back(late).reshape(-1, n, group, width)
            middle_sums, late_sums = halve(middle_value, masks)[:, 0], halve(late_value, masks)[:, 0]
            sums = jnp.concatenate([first_value, middle_sums, late_sums])
            back = [
                lax.ppermute(
                    pick(sums, slot((t + m) % n)),
                    ("dp", "tensor"),
                    [(a * n + b, ((a + b + m) % n) * n + a) for a in range(n) for b in range(n)],
                )
                for m in range(n)
            ]
            returned = jnp.concatenate(
                [lax.select_n((i - t - q) % n, *back) for q in range(n)], axis=0
            )
            token_gradient = (returned.astype(F32) + adapter_backward).astype(BF16)

        with jax.named_scope("tables"):
            *loads, sums = after((*loads, sums))
            grads = [value[:rows] for value in loads]
            parcels = [
                value[rows : value.shape[0] - spare].reshape(blocks_here, -1, width) for value in loads
            ]
            parcels = jnp.stack(parcels)
            parcel = jnp.concatenate([pick(parcels, slot((g - i) % n)) for g in range(n)], axis=0)
            blocks = parcel.shape[0]
            ids = parcel[:, rank, 0].astype(jnp.int32)
            all_shrunk = parcel[:, rank + 1 :].reshape(n, blocks_here, rank, BLOCK)
            shape = (ADAPTER_COUNT, rank, blocks, rank)
            hits = (
                (lax.broadcasted_iota(jnp.int32, shape, 0) == ids[None, None, :, None])
                & (
                    lax.broadcasted_iota(jnp.int32, shape, 1)
                    == lax.broadcasted_iota(jnp.int32, shape, 3)
                )
            ).astype(BF16)
            hits = hits.reshape(ADAPTER_COUNT * rank, blocks * rank)

            def table(products):
                return jnp.dot(
                    hits,
                    products.reshape(blocks * rank, products.shape[-1]),
                    preferred_element_type=F32,
                ).reshape(ADAPTER_COUNT, rank, products.shape[-1])

            grad_down = table(parcel[:, :rank])
            up_products = jnp.stack(
                [
                    (
                        2.0
                        * jnp.einsum(
                            "brk,bkq->brq",
                            pick(all_shrunk, (i + distance(at)) % n),
                            held.reshape(blocks_here, BLOCK, columns),
                            preferred_element_type=F32,
                        )
                    ).astype(BF16)
                    for at, held in enumerate(grads)
                ]
            )
            grad_up = table(
                jnp.concatenate([pick(up_products, slot((g - i) % n)) for g in range(n)], axis=0)
            )
        return (query, token_gradient, grad_down, grad_up)

    return local


def solution(mesh):
    assert mesh.shape["dp"] == mesh.shape["tensor"]
    return jax.shard_map(
        make_local(mesh.shape["tensor"]),
        mesh=mesh,
        in_specs=(
            P(("parts", "dp"), "tensor"),
            P("dp", "tensor"),
            P("parts", None, "tensor"),
            P("parts", None, "tensor"),
            P(("parts", "dp"), "tensor"),
            P(("parts", "dp")),
            P(("parts", "dp")),
        ),
        out_specs=(
            P(("parts", "dp"), "tensor"),
            P(("parts", "dp"), "tensor"),
            P("parts", None, "tensor"),
            P("parts", None, "tensor"),
        ),
        check_vma=False,
    )
```

```python
import jax
import jax.numpy as jnp
from jax import lax
from jax.sharding import PartitionSpec as P

ADAPTER_COUNT = 32
BLOCK = 128
F32 = jnp.float32
BF16 = jnp.bfloat16


def pick(stacked, index):
    return lax.dynamic_index_in_dim(stacked, index, 0, keepdims=False)


def after(values, *earlier):
    return lax.optimization_barrier((tuple(values), earlier))[0]


def make_local(n):
    masks = []
    while 2 ** len(masks) < n:
        masks.append(2 ** len(masks))

    def swap(x, mask):
        return lax.ppermute(x, "tensor", [(t, t ^ mask) for t in range(n)])

    def rotate(x, k):
        return lax.ppermute(x, "dp", [(i, (i + k) % n) for i in range(n)])

    def local(
        tokens,
        query_weight,
        down_weights,
        up_weights,
        cotangent,
        adapter_of_block,
        block_live_count,
    ):
        blocks_here = adapter_of_block.shape[0]
        rows, width = tokens.shape
        columns = query_weight.shape[1]
        rank = down_weights.shape[1]
        group = rows // n
        t = lax.axis_index("tensor")
        i = lax.axis_index("dp")
        half = n // 2
        lower = i < half

        positions = lax.broadcasted_iota(jnp.int32, (blocks_here, BLOCK), 1)
        live_mask = positions < block_live_count[:, None]
        grad_blocks = jnp.where(
            live_mask[:, :, None],
            cotangent.reshape(blocks_here, BLOCK, columns),
            jnp.zeros((), cotangent.dtype),
        )
        grad_flat = grad_blocks.reshape(rows, columns)

        def hop(s, rising, falling):
            with jax.named_scope("spread_cotangent"):
                return (
                    lax.ppermute(rising, "dp", [(a, a + 1) for a in range(s - 1, n - 1)]),
                    lax.ppermute(falling, "dp", [(a + 1, a) for a in range(n - s)]),
                )

        with jax.named_scope("spread_tokens"):
            pieces = lax.all_to_all(
                tokens.reshape(n, group, width), "tensor", 0, 0
            )

        with jax.named_scope("ranks"):
            token_blocks = tokens.reshape(blocks_here, BLOCK, width)
            chosen_down = down_weights[adapter_of_block]
            chosen_up = up_weights[adapter_of_block]
            ranks = jnp.stack(
                [
                    jnp.einsum(
                        "uqv,upv->upq", token_blocks, chosen_down, preferred_element_type=F32
                    ),
                    2.0
                    * jnp.einsum("bkq,brq->brk", grad_blocks, chosen_up, preferred_element_type=F32),
                ]
            )
            for mask in masks:
                ranks = ranks + swap(ranks, mask)
            ranks = ranks.astype(BF16)
            shrunk, grad_rank = ranks[0], ranks[1]
            adapter_output = 2.0 * jnp.einsum(
                "psw,psd->pwd", shrunk, chosen_up, preferred_element_type=F32
            ).reshape(rows, columns)
            adapter_backward = jnp.einsum(
                "jxq,jxo->jqo", grad_rank, chosen_down, preferred_element_type=F32
            ).reshape(rows, width)
            (adapter_backward,) = after((adapter_backward,))

        with jax.named_scope("tables"):
            down_products = jnp.einsum(
                "pgz,pzq->pgq", grad_rank, token_blocks, preferred_element_type=F32
            ).astype(BF16)
            ids = jnp.broadcast_to(
                adapter_of_block[:, None, None].astype(BF16), (blocks_here, 1, width)
            )
            parcel = jnp.concatenate(
                [down_products, ids, shrunk.reshape(blocks_here, -1, width)], axis=1
            )

        spare = -blocks_here * parcel.shape[1] % 16
        load = jnp.concatenate(
            [
                grad_flat,
                parcel.reshape(-1, width),
                jnp.zeros((spare, width), BF16),
            ]
        )
        up, down = {}, {}
        up[1], down[1] = hop(1, load, load)

        with jax.named_scope("spread_tokens"):
            distances = sorted(range(1, n), key=lambda k: -abs(2 * k - n))
            by_source = {0: pick(pieces, i)}
            for k in distances:
                by_source[n - k] = rotate(pick(pieces, (i + k) % n), k)
            near = [n - k for k in distances if k in (1, n - 1)]
            rest = [r for r in range(n) if r not in near]
            full = {}
            for batch in (near, rest):
                held = jnp.stack([by_source[r] for r in batch])
                for at, mask in enumerate(reversed(masks)):
                    other = swap(held, mask)
                    odd = (t // mask) % 2 == 1
                    held = jnp.stack(
                        [jnp.where(odd, other, held), jnp.where(odd, held, other)], axis=1 + at
                    )
                for at, r in enumerate(batch):
                    full[r] = held[at].reshape(rows, width)

        with jax.named_scope("forward"):

            def project(r):
                return jnp.dot(full[r], query_weight, preferred_element_type=F32)

            parts = dict(zip(near, after([project(r).astype(BF16) for r in near])))
            near_parts = tuple(parts.values())
            for r in rest:
                if r != 0:
                    (parts[r],) = after((project(r).astype(BF16),), *near_parts)
            (own,) = after((project(0) + adapter_output,), *near_parts, *parts.values())

        def pull_back(batch):
            return lax.dot_general(
                jnp.concatenate([value[:rows] for value in batch]),
                query_weight,
                (((1,), (1,)), ((), ())),
                preferred_element_type=F32,
            ).astype(BF16)

        def halve(value, masks_here):
            for mask in masks_here:
                count = value.shape[0]
                halves = value.reshape(count, value.shape[1] // 2, 2, group, width)
                bit = (t // mask) % 2
                value = lax.dynamic_index_in_dim(halves, bit, 2, keepdims=False) + swap(
                    lax.dynamic_index_in_dim(halves, 1 - bit, 2, keepdims=False), mask
                )
            return value

        up_sum = down_sum = None
        for s in range(1, n):
            d = n - s
            with jax.named_scope("forward"):
                sends = (
                    (parts[d], parts[n - d])
                    if s == 1
                    else (parts[d] + up_sum, parts[n - d] + down_sum)
                )
                if s == 2:
                    first = after([load, jnp.where(lower, down[1], up[1])], own)
                    first_value = pull_back(first).reshape(-1, n, group, width)
                    *sends, first_value = after((*sends, first_value))
                    first_value = halve(first_value, masks)[:, 0]
                if s == n - 1:
                    middle = after(
                        [jnp.where(lower, down[r], up[r]) for r in range(2, half + 1)], own
                    )
                    middle_value = pull_back(middle).reshape(-1, n, group, width)
                    *sends, middle_value = after((*sends, middle_value))
                up_sum = lax.ppermute(sends[0], "dp", [(a, a + 1) for a in range(s)])
                down_sum = lax.ppermute(sends[1], "dp", [(a, a - 1) for a in range(d, n)])
            up[s], down[s] = after((up[s], down[s]), *(near_parts if s == 1 else sends))
            if s < n - 1:
                up[s + 1], down[s + 1] = hop(s + 1, up[s], down[s])
        with jax.named_scope("forward"):
            query = (own + up_sum.astype(F32) + down_sum.astype(F32)).astype(BF16)

        def slot(r):
            k = jnp.minimum(r, n - r)
            return jnp.where((r == 0) | (r == half), r, jnp.where((r < half) == lower, k, half + k))

        def distance(at):
            if at <= half:
                return jnp.where(lower, at, (n - at) % n)
            return jnp.where(lower, n + half - at, at - half)

        late = [
            jnp.where(
                lower,
                jnp.where(i >= r, up[r], down[n - r]),
                jnp.where(i + r <= n - 1, down[r], up[n - r]),
            )
            for r in range(1, half)
        ]
        loads = [*first, *middle, *late]

        with jax.named_scope("backward"):
            late_value = pull_back(late).reshape(-1, n, group, width)
            middle_sums, late_sums = halve(middle_value, masks)[:, 0], halve(late_value, masks)[:, 0]
            sums = jnp.concatenate([first_value, middle_sums, late_sums])
            back = [
                lax.ppermute(
                    pick(sums, slot((t + m) % n)),
                    ("dp", "tensor"),
                    [(a * n + b, ((a + b + m) % n) * n + a) for a in range(n) for b in range(n)],
                )
                for m in range(n)
            ]
            returned = jnp.concatenate(
                [lax.select_n((i - t - q) % n, *back) for q in range(n)], axis=0
            )
            token_gradient = (returned.astype(F32) + adapter_backward).astype(BF16)

        with jax.named_scope("tables"):
            *loads, sums = after((*loads, sums))
            grads = [value[:rows] for value in loads]
            parcels = [
                value[rows : value.shape[0] - spare].reshape(blocks_here, -1, width) for value in loads
            ]
            parcels = jnp.stack(parcels)
            parcel = jnp.concatenate([pick(parcels, slot((g - i) % n)) for g in range(n)], axis=0)
            blocks = parcel.shape[0]
            ids = parcel[:, rank, 0].astype(jnp.int32)
            all_shrunk = parcel[:, rank + 1 :].reshape(n, blocks_here, rank, BLOCK)
            shape = (ADAPTER_COUNT, rank, blocks, rank)
            hits = (
                (lax.broadcasted_iota(jnp.int32, shape, 0) == ids[None, None, :, None])
                & (
                    lax.broadcasted_iota(jnp.int32, shape, 1)
                    == lax.broadcasted_iota(jnp.int32, shape, 3)
                )
            ).astype(BF16)
            hits = hits.reshape(ADAPTER_COUNT * rank, blocks * rank)

            def table(products):
                return jnp.dot(
                    hits,
                    products.reshape(blocks * rank, products.shape[-1]),
                    preferred_element_type=F32,
                ).reshape(ADAPTER_COUNT, rank, products.shape[-1])

            grad_down = table(parcel[:, :rank])
            up_products = jnp.stack(
                [
                    (
                        2.0
                        * jnp.einsum(
                            "brk,bkq->brq",
                            pick(all_shrunk, (i + distance(at)) % n),
                            held.reshape(blocks_here, BLOCK, columns),
                            preferred_element_type=F32,
                        )
                    ).astype(BF16)
                    for at, held in enumerate(grads)
                ]
            )
            grad_up = table(
                jnp.concatenate([pick(up_products, slot((g - i) % n)) for g in range(n)], axis=0)
            )
        return (query, token_gradient, grad_down, grad_up)

    return local


def solution(mesh):
    assert mesh.shape["dp"] == mesh.shape["tensor"]
    return jax.shard_map(
        make_local(mesh.shape["tensor"]),
        mesh=mesh,
        in_specs=(
            P(("parts", "dp"), "tensor"),
            P("dp", "tensor"),
            P("parts", None, "tensor"),
            P("parts", None, "tensor"),
            P(("parts", "dp"), "tensor"),
            P(("parts", "dp")),
            P(("parts", "dp")),
        ),
        out_specs=(
            P(("parts", "dp"), "tensor"),
            P(("parts", "dp"), "tensor"),
            P("parts", None, "tensor"),
            P("parts", None, "tensor"),
        ),
        check_vma=False,
    )
```
